256 devices in a mesh: gx: 8 (over x, core), gyz: 8 (over y, z_lo), band: 4 (over z_hi).
Axes of the slice: x: 4, y: 4, z: 8 (z_hi: 4, z_lo: 2; z = z_hi * 2 + z_lo), core: 2. Of those that a mesh axis runs over, the one named last changes fastest.
Arguments:
- orbitals: float32 [256, 32, 64, 128], P('band', 'gx', 'gyz'), may hold values from -6 to 6
- v_local: float32 [32, 64, 128], P('gx', 'gyz'), may hold values from 0 to 2
- features: bfloat16 [11, 32, 64, 128], P(None, 'gx', 'gyz'), may hold values from -6 to 6
- w_first: bfloat16 [256, 11], replicated, may hold values from -1.75 to 1.75
- w_hidden: bfloat16 [1, 256, 256], replicated, may hold values from -0.375 to 0.375
- w_last: bfloat16 [256], replicated, may hold values from -0.375 to 0.375
- rotation: float32 [256, 256], replicated, may hold values from -0.375 to 0.375
- assignment: int32 [256], replicated, may hold values from 0 to 255, each once
- degrees: int32 [256], P('band'), may hold values from 4 to 8, as said below
Outputs:
- gram: float32 [256, 256], P('band')
- rotated: float32 [256, 32, 64, 128], P('band', 'gx', 'gyz')
The draws below stay inside these ranges and needn't reach their ends.
Inputs may be any that keep to these rules, and one draw needn't show every extreme that they name: `degrees`: a filter degree of each slot; some slot has 8 and some has 4. `assignment`: each orbital is held in exactly one slot.
All inputs are finite; a program needn't handle non-finite values.
Results may differ from the reference program's by a relative error of at most 0.0043.
Values may be sent and summed in bfloat16 or wider, within the bound.
No kernel may reach another device: no remote copies, remote signals or barrier semaphores. Data moves between devices by JAX's collectives and lax.ppermute only.
A program may use at most 64 MiB of HBM per device.

```python
import math
import jax
import jax.numpy as jnp
from jax import lax

NZ = 128
NB = 256
H = 256
F = 11
LAYERS = 2
DEG = 8
NX = 32
NY = 64


def draw_degrees(key, part):
    key_values = jax.random.fold_in(key, 11)
    key_high = jax.random.fold_in(key, 12)
    key_low = jax.random.fold_in(key, 13)
    values = jax.random.randint(key_values, (NB,), DEG // 2, DEG + 1)
    high_slot = jax.random.randint(key_high, (), 0, NB)
    low_slot = (high_slot + 1 + jax.random.randint(key_low, (), 0, NB - 1)) % NB
    values = values.at[high_slot].set(DEG)
    values = values.at[low_slot].set(DEG // 2)
    return values.astype(jnp.int32)


def level_of(stream_key, shape, pieces, smallest, top_value):
    level = 1.0
    for position, blocks in pieces:
        heights = jax.random.uniform(jax.random.fold_in(jax.random.fold_in(stream_key, 6), position), (blocks,), jnp.float32, smallest / len(pieces), top_value / len(pieces))
        level = level * jnp.repeat(jnp.exp(heights), shape[position] // blocks).reshape((-1,) + (1,) * (len(shape) - 1 - position))
    return level


def bell_draw(own_key, shape, spread, bound, cuts=(), held_as=jnp.bfloat16):
    factor_of = level_of(own_key, shape, cuts, -0.22, 0.18) if cuts else 1.0
    result = jax.random.normal(own_key, shape, jnp.float32) * spread * factor_of
    return jnp.minimum(jnp.maximum(result, -bound), bound).astype(held_as)


def setup_inputs(seed: int = 0) -> dict:
    seeds = jax.random.split(jax.random.key(seed), 10)
    return {
        "orbitals": bell_draw(seeds[0], (NB, NX, NY, NZ), 1.0, 6.0, ((0, 4), (1, 8), (2, 8)), jnp.float32),
        "v_local": jnp.clip(2.0 * jax.random.uniform(seeds[1], (NX, NY, NZ), jnp.float32) ** level_of(seeds[1], (NX, NY, NZ), ((0, 8), (1, 8)), -0.2, 0.2), 0.0, 2.0),
        "features": bell_draw(seeds[2], (F, NX, NY, NZ), 1.0, 6.0, ((1, 8), (2, 8))),
        "w_first": bell_draw(seeds[3], (H, F), F ** -0.5, 1.75),
        "w_hidden": bell_draw(seeds[4], (LAYERS - 1, H, H), H ** -0.5, 0.375),
        "w_last": bell_draw(seeds[5], (H,), H ** -0.5, 0.375),
        "rotation": bell_draw(seeds[6], (NB, NB), NB ** -0.5, 0.375, (), jnp.float32),
        "assignment": jax.random.permutation(seeds[7], NB).astype(jnp.int32),
        "degrees": draw_degrees(jax.random.fold_in(seeds[9], 71), 0),
    }


LOWER_EDGE = 2.0
CUT_EDGE = 3.0
UPPER_EDGE = 9.5


def coefficients(count):
    half_width = (UPPER_EDGE - CUT_EDGE) / 2.0
    centre = (UPPER_EDGE + CUT_EDGE) / 2.0
    first = half_width / (LOWER_EDGE - centre)
    factors = [(first / half_width, 0.0)]
    sigma = first
    for rounds in range(1, count):
        updated = 1.0 / (2.0 / first - sigma)
        factors.append((2.0 * updated / half_width, sigma * updated))
        sigma = updated
    return factors, centre


def hamiltonian(field, potential):
    padded = jnp.pad(field, ((0, 0), (1, 1), (1, 1), (1, 1)))
    beside_all = padded[:, 2:, 1:-1, 1:-1] + padded[:, :-2, 1:-1, 1:-1]
    beside_all = beside_all + padded[:, 1:-1, 2:, 1:-1] + padded[:, 1:-1, :-2, 1:-1]
    beside_all = beside_all + padded[:, 1:-1, 1:-1, 2:] + padded[:, 1:-1, 1:-1, :-2]
    return 0.5 * (6.0 * field - beside_all) + potential * field


def chebyshev(field, potential, slot_degrees):
    factors, centre = coefficients(DEG)
    previous = field
    current = field
    for rounds in range(DEG):
        image = hamiltonian(current, potential)
        scale_new, scale_old = factors[rounds]
        updated = scale_new * (image - centre * current) - scale_old * previous
        active = (slot_degrees > rounds)[:, None, None, None]
        previous = jnp.where(active, current, previous)
        current = jnp.where(active, updated, current)
    return current


def network(flattened, w_first, w_hidden, w_last):
    hidden = jax.nn.silu(jnp.dot(w_first, flattened, preferred_element_type=jnp.float32)).astype(jnp.bfloat16)
    for section in range(LAYERS - 1):
        hidden = jax.nn.silu(jnp.dot(w_hidden[section], hidden, preferred_element_type=jnp.float32)).astype(jnp.bfloat16)
    return jnp.tanh(jnp.dot(w_last[None, :], hidden, preferred_element_type=jnp.float32)[0])


def reference(orbitals, v_local, features, w_first, w_hidden, w_last, rotation, assignment, degrees):
    def plane_potential(plane):
        return network(plane.reshape(F, NY * NZ), w_first, w_hidden, w_last).reshape(NY, NZ)

    xc_field = lax.map(plane_potential, jnp.moveaxis(features, 1, 0))
    potential = v_local + xc_field
    group = math.gcd(NB, 16)
    blocks = orbitals.reshape(NB // group, group, NX, NY, NZ)
    block_degrees = degrees.reshape(NB // group, group)

    def filter_block(pair):
        return chebyshev(pair[0], potential, pair[1]).astype(jnp.bfloat16)

    filtered = lax.map(filter_block, (blocks, block_degrees)).reshape(NB, NX * NY * NZ)
    gram = jnp.dot(filtered, filtered.T, preferred_element_type=jnp.float32) / float(NX * NY * NZ)
    slot_rotation = rotation[assignment][:, assignment].astype(jnp.bfloat16)
    rotated = jnp.dot(slot_rotation.T, filtered, preferred_element_type=jnp.float32)
    return gram, rotated.reshape(NB, NX, NY, NZ)
```

```python
import jax
import jax.numpy as jnp
from jax import lax
from jax.experimental import pallas as pl
from jax.experimental.pallas import tpu as pltpu
from jax.sharding import PartitionSpec as P

DEG = 8


LOWER_EDGE = 2.0
CUT_EDGE = 3.0
UPPER_EDGE = 9.5


def coefficients(count):
    half_width = (UPPER_EDGE - CUT_EDGE) / 2.0
    centre = (UPPER_EDGE + CUT_EDGE) / 2.0
    first = half_width / (LOWER_EDGE - centre)
    factors = [(first / half_width, 0.0)]
    sigma = first
    for rounds in range(1, count):
        updated = 1.0 / (2.0 / first - sigma)
        factors.append((2.0 * updated / half_width, sigma * updated))
        sigma = updated
    return (factors, centre)


def network(cell_features, w_first, w_hidden, w_last):
    feature_count = cell_features.shape[0]
    flattened = cell_features.reshape(feature_count, -1)
    hidden = jax.nn.silu(jnp.dot(w_first, flattened, preferred_element_type=jnp.float32)).astype(
        jnp.bfloat16
    )
    hidden = jax.nn.silu(jnp.dot(w_hidden[0], hidden, preferred_element_type=jnp.float32)).astype(
        jnp.bfloat16
    )
    values = jnp.tanh(jnp.dot(w_last[None, :], hidden, preferred_element_type=jnp.float32)[0])
    return values.reshape(cell_features.shape[1:])


NX, NY, NZ = 32, 64, 128
PAD = 8


def filter_kernel(info, taken, other, out, field, shifted):
    factors, centre = coefficients(DEG)
    core = info[0]
    degree = info[1]
    edge = jnp.zeros((NY + 2 * PAD, NZ), jnp.float32)
    rim = jnp.zeros((PAD, NZ), jnp.float32)
    for which in range(2):
        field[which, 0] = edge
        field[which, NX + 1] = edge

    def load(plane, carry):
        outer = lax.div(plane, 4)
        inner = lax.rem(plane, 4)
        half = lax.div(inner, 2)
        place = lax.rem(inner, 2)
        for which in range(2):
            field[which, plane + 1, 0:PAD] = rim
            field[which, plane + 1, PAD + NY :] = rim
        for run in range(8):
            rows = slice(PAD + 8 * run, PAD + 8 * run + 8)
            block = taken[outer * 8 + run, inner]
            field[0, plane + 1, rows] = block
            field[1, plane + 1, rows] = block
            own = taken[outer * 8 + run, 4 + place]
            far = other[outer * 8 + run, place]
            value = jnp.where(half == core, own, far)
            shifted[plane, 8 * run : 8 * run + 8] = value + (3.0 - centre)
        return carry

    lax.fori_loop(0, NX, load, 0)
    lane = lax.broadcasted_iota(jnp.int32, (NY, NZ), 1)
    not_first = lane > 0
    not_last = lane < NZ - 1
    for rounds in range(DEG):
        scale_new, scale_old = factors[rounds]
        now = rounds % 2
        then = 1 - now

        @pl.when(rounds < degree)
        def _():
            def step(plane, carry):
                x = plane + 1
                here = field[now, x, PAD : PAD + NY]
                beside = field[now, x - 1, PAD : PAD + NY] + field[now, x + 1, PAD : PAD + NY]
                beside += (
                    field[now, x, PAD - 1 : PAD + NY - 1] + field[now, x, PAD + 1 : PAD + NY + 1]
                )
                beside += jnp.where(not_first, pltpu.roll(here, 1, 1), 0.0)
                beside += jnp.where(not_last, pltpu.roll(here, NZ - 1, 1), 0.0)
                fresh = scale_new * (shifted[plane] * here - 0.5 * beside)
                if scale_old != 0.0:
                    fresh -= scale_old * field[then, x, PAD : PAD + NY]
                field[then, x, PAD : PAD + NY] = fresh
                return carry

            lax.fori_loop(0, NX, step, 0)

    last = lax.rem(degree, 2)

    def store(plane, carry):
        out[lax.rem(plane, 4), lax.div(plane, 4)] = field[last, plane + 1, PAD : PAD + NY].astype(
            jnp.bfloat16
        )
        return carry

    lax.fori_loop(0, NX, store, 0)


def run_filter(info, taken, other):
    vmem = pl.BlockSpec(memory_space=pltpu.VMEM)
    return pl.pallas_call(
        filter_kernel,
        out_shape=jax.ShapeDtypeStruct((4, 8, NY, NZ), jnp.bfloat16),
        in_specs=[pl.BlockSpec(memory_space=pltpu.SMEM), vmem, vmem],
        out_specs=vmem,
        scratch_shapes=[
            pltpu.VMEM((2, NX + 2, NY + 2 * PAD, NZ), jnp.float32),
            pltpu.VMEM((NX, NY, NZ), jnp.float32),
        ],
        compiler_params=pltpu.CompilerParams(vmem_limit_bytes=24 * 1024 * 1024),
        cost_estimate=pl.CostEstimate(
            flops=8 * 16 * NX * NY * NZ, bytes_accessed=3 * 1024 * 1024, transcendentals=0
        ),
    )(info, taken, other)


def reduce_over(value, axis, step, count):
    size = lax.axis_size(axis)
    total = value
    for shift in range(1, count):
        pairs = []
        for i in range(size):
            place = (i // step) % count
            pairs.append((i, i + (((place + shift) % count) - place) * step))
        total = total + lax.ppermute(value, axis, pairs)
    return total


def on_device(
    orbitals, v_local, features, w_first, w_hidden, w_last, rotation, assignment, degrees
):
    band = lax.axis_index("band")
    gx = lax.axis_index("gx")
    gyz = lax.axis_index("gyz")
    total_slots = rotation.shape[0]
    local_slots, size_x, size_y, size_z = orbitals.shape
    total_cells = float(NX * NY * NZ)

    potential = v_local + network(features, w_first, w_hidden, w_last)
    halves = potential.reshape(1, 2, 1, 2, size_y, size_z)
    halves = jnp.broadcast_to(halves, (4, 2, 8, 2, size_y, size_z)).reshape(64, 2, size_y, size_z)
    message = jnp.concatenate([orbitals, halves], axis=1)
    taken = lax.all_to_all(message, ("gx", "gyz"), 0, 0, tiled=True)
    other = lax.ppermute(taken[:, 4:], "gx", [(i, i ^ 1) for i in range(8)])
    degree = lax.dynamic_index_in_dim(degrees, gx * 8 + gyz, 0, keepdims=False)
    info = jnp.stack([lax.rem(gx, 2), degree]).astype(jnp.int32)
    filtered = run_filter(info, taken, other)

    select = (assignment[:, None] == lax.iota(jnp.int32, total_slots)[None, :]).astype(jnp.bfloat16)
    permuted = jnp.dot(
        select, rotation.astype(jnp.bfloat16), preferred_element_type=jnp.float32
    ).astype(jnp.bfloat16)
    slot_rotation = jnp.dot(permuted, select.T, preferred_element_type=jnp.float32).astype(
        jnp.bfloat16
    )

    panel = lax.all_to_all(
        filtered.reshape(256, 8, 128), ("band", "gx", "gyz"), 0, 0, tiled=True
    ).reshape(256, 1024)
    margin = lax.dot_general(
        panel, panel, (((1,), (1,)), ((), ())), preferred_element_type=jnp.float32
    )
    turned = lax.dot_general(
        slot_rotation, panel, (((0,), (0,)), ((), ())), preferred_element_type=jnp.float32
    ).astype(jnp.bfloat16)

    rows = margin.reshape(4, local_slots, total_slots)
    gram = lax.dynamic_index_in_dim(rows, band, 0, keepdims=False)
    for shift in range(1, 4):
        piece = lax.dynamic_index_in_dim(rows, lax.rem(band + shift, 4), 0, keepdims=False)
        gram = gram + lax.ppermute(piece, "band", [(i, (i + shift) % 4) for i in range(4)])
    gram = reduce_over(gram, "gx", 1, 2)
    gram = reduce_over(gram, "gyz", 1, 2)
    gram = reduce_over(gram, "gx", 2, 4)
    gram = reduce_over(gram, "gyz", 2, 4) / total_cells

    back = lax.all_to_all(turned.reshape(4, local_slots, 1024), "band", 0, 0, tiled=True)
    rotated = jnp.swapaxes(back, 0, 1).reshape(local_slots, size_x, size_y, size_z)
    return (gram, rotated.astype(jnp.float32))


def solution(mesh):
    placed = (
        P("band", "gx", "gyz", None),
        P("gx", "gyz", None),
        P(None, "gx", "gyz", None),
        P(),
        P(),
        P(),
        P(),
        P(),
        P("band"),
    )
    return jax.shard_map(
        on_device,
        mesh=mesh,
        in_specs=placed,
        out_specs=(P("band", None), P("band", "gx", "gyz", None)),
        check_vma=False,
    )
```

```python
import jax
import jax.numpy as jnp
from jax import lax
from jax.experimental import pallas as pl
from jax.experimental.pallas import tpu as pltpu
from jax.sharding import PartitionSpec as P

DEG = 8


LOWER_EDGE = 2.0
CUT_EDGE = 3.0
UPPER_EDGE = 9.5


def coefficients(count):
    half_width = (UPPER_EDGE - CUT_EDGE) / 2.0
    centre = (UPPER_EDGE + CUT_EDGE) / 2.0
    first = half_width / (LOWER_EDGE - centre)
    factors = [(first / half_width, 0.0)]
    sigma = first
    for rounds in range(1, count):
        updated = 1.0 / (2.0 / first - sigma)
        factors.append((2.0 * updated / half_width, sigma * updated))
        sigma = updated
    return (factors, centre)


def network(cell_features, w_first, w_hidden, w_last):
    feature_count = cell_features.shape[0]
    flattened = cell_features.reshape(feature_count, -1)
    hidden = jax.nn.silu(jnp.dot(w_first, flattened, preferred_element_type=jnp.float32)).astype(
        jnp.bfloat16
    )
    hidden = jax.nn.silu(jnp.dot(w_hidden[0], hidden, preferred_element_type=jnp.float32)).astype(
        jnp.bfloat16
    )
    values = jnp.tanh(
        jnp.dot(
            jnp.broadcast_to(w_last, (8, w_last.shape[0])),
            hidden,
            preferred_element_type=jnp.float32,
        )[0]
    )
    return values.reshape(cell_features.shape[1:])


NX, NY, NZ = 32, 64, 128
PAD = 8
TOGETHER = 16
ORBITAL_SCALE = 8192.0
POTENTIAL_MIDDLE = 1.0


def filter_kernel(info, taken, other, out, field, shifted):
    factors, centre = coefficients(DEG)
    core = info[0]
    degree = info[1]
    edge = jnp.zeros((NY + 2 * PAD, NZ), jnp.float32)
    rim = jnp.zeros((PAD, NZ), jnp.float32)
    for which in range(2):
        field[which, 0] = edge
        field[which, NX + 1] = edge

    def load(outer, carry):
        for inner in range(4):
            plane = outer * 4 + inner
            for which in range(2):
                field[which, plane + 1, 0:PAD] = rim
                field[which, plane + 1, PAD + NY :] = rim
            for run in range(8):
                rows = slice(PAD + 8 * run, PAD + 8 * run + 8)
                field[0, plane + 1, rows] = taken[outer * 8 + run, inner] * (1.0 / ORBITAL_SCALE)
                own = taken[outer * 8 + run, 4 + inner % 2]
                far = other[outer * 8 + run, inner % 2]
                value = jnp.where(inner // 2 == core, own, far)
                shifted[plane, 8 * run : 8 * run + 8] = value + (POTENTIAL_MIDDLE + 3.0 - centre)
        return carry

    lax.fori_loop(0, NX // 4, load, 0)
    lane = lax.broadcasted_iota(jnp.int32, (8, NZ), 1)
    not_first = lane > 0
    not_last = lane < NZ - 1

    def tile(now, then, x, row, scale_new, scale_old):
        low = PAD + row
        here = field[now, x, low : low + 8]
        beside = field[now, x - 1, low : low + 8] + field[now, x + 1, low : low + 8]
        beside += field[now, x, low - 1 : low + 7] + field[now, x, low + 1 : low + 9]
        beside += jnp.where(not_first, pltpu.roll(here, 1, 1), 0.0) + jnp.where(
            not_last, pltpu.roll(here, NZ - 1, 1), 0.0
        )
        fresh = (scale_new * shifted[x - 1, row : row + 8]) * here - (0.5 * scale_new) * beside
        if scale_old != 0.0:
            fresh -= scale_old * field[then, x, low : low + 8]
        field[then, x, low : low + 8] = fresh

    for rounds in range(DEG):
        scale_new, scale_old = factors[rounds]
        now = rounds % 2

        @pl.when(rounds < degree)
        def _():
            def step(turn, carry):
                for part in range(TOGETHER):
                    for row in range(0, NY, 8):
                        tile(now, 1 - now, turn * TOGETHER + part + 1, row, scale_new, scale_old)
                return carry

            lax.fori_loop(0, NX // TOGETHER, step, 0)

    last = lax.rem(degree, 2)

    def store(outer, carry):
        for inner in range(4):
            out[inner, outer] = field[last, outer * 4 + inner + 1, PAD : PAD + NY].astype(
                jnp.bfloat16
            )
        return carry

    lax.fori_loop(0, NX // 4, store, 0)


ACROSS = [(i, i ^ 1) for i in range(8)]


def run_filter(info, taken, other):
    vmem = pl.BlockSpec(memory_space=pltpu.VMEM)
    return pl.pallas_call(
        filter_kernel,
        out_shape=jax.ShapeDtypeStruct((4, 8, NY, NZ), jnp.bfloat16),
        in_specs=[pl.BlockSpec(memory_space=pltpu.SMEM), vmem, vmem],
        out_specs=vmem,
        scratch_shapes=[
            pltpu.VMEM((2, NX + 2, NY + 2 * PAD, NZ), jnp.float32),
            pltpu.VMEM((NX, NY, NZ), jnp.float32),
        ],
        compiler_params=pltpu.CompilerParams(vmem_limit_bytes=24 * 1024 * 1024),
        cost_estimate=pl.CostEstimate(
            flops=8 * 16 * NX * NY * NZ, bytes_accessed=3 * 1024 * 1024, transcendentals=0
        ),
    )(info, taken, other)


def reduce_over(value, axis, step, count):
    size = lax.axis_size(axis)
    total = value
    for shift in range(1, count):
        pairs = []
        for i in range(size):
            place = (i // step) % count
            pairs.append((i, i + (((place + shift) % count) - place) * step))
        total = total + lax.ppermute(value, axis, pairs)
    return total


def on_device(
    orbitals, v_local, features, w_first, w_hidden, w_last, rotation, assignment, degrees
):
    band = lax.axis_index("band")
    gx = lax.axis_index("gx")
    gyz = lax.axis_index("gyz")
    total_slots = rotation.shape[0]
    local_slots, size_x, size_y, size_z = orbitals.shape
    total_cells = float(NX * NY * NZ)

    potential = v_local + network(features, w_first, w_hidden, w_last)
    halves = potential.reshape(1, 2, 1, 2, size_y, size_z)
    halves = jnp.broadcast_to(halves, (4, 2, 8, 2, size_y, size_z)).reshape(64, 2, size_y, size_z)
    message = jnp.concatenate([orbitals * ORBITAL_SCALE, halves - POTENTIAL_MIDDLE], axis=1)
    message = message.astype(jnp.float16)
    core = lax.rem(gx, 2)
    degree = lax.dynamic_index_in_dim(degrees, gx * 8 + gyz, 0, keepdims=False)
    info = jnp.stack([core, degree]).astype(jnp.int32)
    taken = lax.all_to_all(message, ("gx", "gyz"), 0, 0, tiled=True)
    other = lax.ppermute(taken[:, 4:], "gx", ACROSS)
    filtered = run_filter(info, taken.astype(jnp.float32), other.astype(jnp.float32))

    select = (assignment[:, None] == lax.iota(jnp.int32, total_slots)[None, :]).astype(jnp.bfloat16)
    permuted = jnp.dot(
        select, rotation.astype(jnp.bfloat16), preferred_element_type=jnp.float32
    ).astype(jnp.bfloat16)
    slot_rotation = jnp.dot(permuted, select.T, preferred_element_type=jnp.float32).astype(
        jnp.bfloat16
    )

    panel = lax.all_to_all(
        filtered.reshape(256, 8, 128), ("band", "gx", "gyz"), 0, 0, tiled=True
    )
    panel, slot_rotation = lax.optimization_barrier((panel, slot_rotation))
    panel = panel.reshape(256, 1024)
    margin = lax.dot_general(
        panel, panel, (((1,), (1,)), ((), ())), preferred_element_type=jnp.float32
    )
    half = total_slots // 2
    kept = jnp.where(core == 0, margin[:, :half], margin[:, half:])
    sent = jnp.where(core == 0, margin[:, half:], margin[:, :half])
    rows = (kept + lax.ppermute(sent, "gx", ACROSS)).reshape(4, local_slots, half)
    rows, panel = lax.optimization_barrier((rows, panel))
    turned = lax.dot_general(
        slot_rotation, panel, (((0,), (0,)), ((), ())), preferred_element_type=jnp.float32
    ).astype(jnp.bfloat16)
    gram = lax.dynamic_index_in_dim(rows, band, 0, keepdims=False)
    for shift in range(1, 4):
        piece = lax.dynamic_index_in_dim(rows, lax.rem(band + shift, 4), 0, keepdims=False)
        gram = gram + lax.ppermute(piece, "band", [(i, (i + shift) % 4) for i in range(4)])
    gram = reduce_over(gram, "gx", 2, 4)
    gram = reduce_over(gram, "gyz", 2, 4)
    back = lax.all_to_all(turned.reshape(4, local_slots, 1024), "band", 0, 0, tiled=True)
    gram = reduce_over(gram, "gyz", 1, 2)
    gram, back = lax.optimization_barrier((gram, back))
    rotated = jnp.swapaxes(back, 0, 1).reshape(local_slots, size_x, size_y, size_z)
    rotated = rotated.astype(jnp.float32)
    beyond = lax.ppermute(gram, "gx", ACROSS)
    gram = (
        jnp.concatenate(
            [jnp.where(core == 0, gram, beyond), jnp.where(core == 0, beyond, gram)], axis=1
        )
        / total_cells
    )
    return (gram, rotated)


def solution(mesh):
    placed = (
        P("band", "gx", "gyz", None),
        P("gx", "gyz", None),
        P(None, "gx", "gyz", None),
        P(),
        P(),
        P(),
        P(),
        P(),
        P("band"),
    )
    return jax.shard_map(
        on_device,
        mesh=mesh,
        in_specs=placed,
        out_specs=(P("band", None), P("band", "gx", "gyz", None)),
        check_vma=False,
    )
```

```python
import jax
import jax.numpy as jnp
from jax import lax
from jax.experimental import pallas as pl
from jax.experimental.pallas import tpu as pltpu
from jax.sharding import PartitionSpec as P

DEG = 8


LOWER_EDGE = 2.0
CUT_EDGE = 3.0
UPPER_EDGE = 9.5


def coefficients(count):
    half_width = (UPPER_EDGE - CUT_EDGE) / 2.0
    centre = (UPPER_EDGE + CUT_EDGE) / 2.0
    first = half_width / (LOWER_EDGE - centre)
    factors = [(first / half_width, 0.0)]
    sigma = first
    for rounds in range(1, count):
        updated = 1.0 / (2.0 / first - sigma)
        factors.append((2.0 * updated / half_width, sigma * updated))
        sigma = updated
    return (factors, centre)


def silu(value):
    half = 0.5 * value
    return (half + half * jnp.tanh(half)).astype(jnp.bfloat16)


def network(cell_features, w_first, w_hidden, w_last):
    feature_count = cell_features.shape[0]
    flattened = cell_features.reshape(feature_count, -1)
    hidden = silu(jnp.dot(w_first, flattened, preferred_element_type=jnp.float32))
    hidden = silu(jnp.dot(w_hidden[0], hidden, preferred_element_type=jnp.float32))
    values = jnp.tanh(
        jnp.dot(
            jnp.broadcast_to(w_last, (8, w_last.shape[0])),
            hidden,
            preferred_element_type=jnp.float32,
        )[0]
    )
    return values.reshape(cell_features.shape[1:])


NX, NY, NZ = 32, 64, 128
PAD = 8
TOGETHER = 32
ORBITAL_SCALE = 8192.0
POTENTIAL_MIDDLE = 1.0


def filter_kernel(info, taken, other, out, field, shifted):
    factors, centre = coefficients(DEG)
    core = info[0]
    degree = info[1]
    edge = jnp.zeros((NY + 2 * PAD, NZ), jnp.float32)
    rim = jnp.zeros((PAD, NZ), jnp.float32)
    for which in range(2):
        field[which, 0] = edge
        field[which, NX + 1] = edge

    def load(outer, carry):
        for inner in range(4):
            plane = outer * 4 + inner
            for which in range(2):
                field[which, plane + 1, 0:PAD] = rim
                field[which, plane + 1, PAD + NY :] = rim
            for run in range(8):
                rows = slice(PAD + 8 * run, PAD + 8 * run + 8)
                field[0, plane + 1, rows] = taken[outer * 8 + run, inner] * (1.0 / ORBITAL_SCALE)
                own = taken[outer * 8 + run, 4 + inner % 2]
                far = other[outer * 8 + run, inner % 2]
                value = jnp.where(inner // 2 == core, own, far)
                shifted[plane, 8 * run : 8 * run + 8] = value + (POTENTIAL_MIDDLE + 3.0 - centre)
        return carry

    lax.fori_loop(0, NX // 4, load, 0)
    lane = lax.broadcasted_iota(jnp.int32, (8, NZ), 1)
    not_first = lane > 0
    not_last = lane < NZ - 1

    def tile(now, then, x, row, scale_new, scale_old):
        low = PAD + row
        here = field[now, x, low : low + 8]
        beside = field[now, x - 1, low : low + 8] + field[now, x + 1, low : low + 8]
        beside += field[now, x, low - 1 : low + 7] + field[now, x, low + 1 : low + 9]
        beside += jnp.where(not_first, pltpu.roll(here, 1, 1), 0.0) + jnp.where(
            not_last, pltpu.roll(here, NZ - 1, 1), 0.0
        )
        fresh = (scale_new * shifted[x - 1, row : row + 8]) * here - (0.5 * scale_new) * beside
        if scale_old != 0.0:
            fresh -= scale_old * field[then, x, low : low + 8]
        field[then, x, low : low + 8] = fresh

    for rounds in range(DEG):
        scale_new, scale_old = factors[rounds]
        now = rounds % 2

        @pl.when(rounds < degree)
        def _():
            def step(turn, carry):
                for part in range(TOGETHER):
                    for row in range(0, NY, 8):
                        tile(now, 1 - now, turn * TOGETHER + part + 1, row, scale_new, scale_old)
                return carry

            lax.fori_loop(0, NX // TOGETHER, step, 0)

    last = lax.rem(degree, 2)

    def store(outer, carry):
        for inner in range(4):
            out[inner, outer] = field[last, outer * 4 + inner + 1, PAD : PAD + NY].astype(
                jnp.bfloat16
            )
        return carry

    lax.fori_loop(0, NX // 4, store, 0)


ACROSS = [(i, i ^ 1) for i in range(8)]


def run_filter(info, taken, other):
    vmem = pl.BlockSpec(memory_space=pltpu.VMEM)
    return pl.pallas_call(
        filter_kernel,
        out_shape=jax.ShapeDtypeStruct((4, 8, NY, NZ), jnp.bfloat16),
        in_specs=[pl.BlockSpec(memory_space=pltpu.SMEM), vmem, vmem],
        out_specs=vmem,
        scratch_shapes=[
            pltpu.VMEM((2, NX + 2, NY + 2 * PAD, NZ), jnp.float32),
            pltpu.VMEM((NX, NY, NZ), jnp.float32),
        ],
        compiler_params=pltpu.CompilerParams(vmem_limit_bytes=24 * 1024 * 1024),
        cost_estimate=pl.CostEstimate(
            flops=8 * 16 * NX * NY * NZ, bytes_accessed=3 * 1024 * 1024, transcendentals=0
        ),
    )(info, taken, other)


def reduce_over(value, axis, step, count):
    size = lax.axis_size(axis)
    total = value
    sent = value.astype(jnp.bfloat16)
    for shift in range(1, count):
        pairs = []
        for i in range(size):
            place = (i // step) % count
            pairs.append((i, i + (((place + shift) % count) - place) * step))
        total = total + lax.ppermute(sent, axis, pairs).astype(value.dtype)
    return total


def to_band(value, shift):
    return lax.ppermute(value, "band", [(i, (i + shift) % 4) for i in range(4)])


def on_device(
    orbitals, v_local, features, w_first, w_hidden, w_last, rotation, assignment, degrees
):
    band = lax.axis_index("band")
    gx = lax.axis_index("gx")
    gyz = lax.axis_index("gyz")
    total_slots = rotation.shape[0]
    local_slots, size_x, size_y, size_z = orbitals.shape
    total_cells = float(NX * NY * NZ)

    potential = v_local + network(features, w_first, w_hidden, w_last)
    halves = potential.reshape(1, 2, 1, 2, size_y, size_z)
    halves = jnp.broadcast_to(halves, (4, 2, 8, 2, size_y, size_z)).reshape(64, 2, size_y, size_z)
    message = jnp.concatenate([orbitals * ORBITAL_SCALE, halves - POTENTIAL_MIDDLE], axis=1)
    message = message.astype(jnp.float16)
    core = lax.rem(gx, 2)
    degree = lax.dynamic_index_in_dim(degrees, gx * 8 + gyz, 0, keepdims=False)
    info = jnp.stack([core, degree]).astype(jnp.int32)
    taken = lax.all_to_all(message, ("gx", "gyz"), 0, 0, tiled=True)
    other = lax.ppermute(taken[:, 4:], "gx", ACROSS)
    filtered = run_filter(info, taken.astype(jnp.float32), other.astype(jnp.float32))

    select = (assignment[:, None] == lax.iota(jnp.int32, total_slots)[None, :]).astype(jnp.bfloat16)
    permuted = jnp.dot(
        select, rotation.astype(jnp.bfloat16), preferred_element_type=jnp.float32
    ).astype(jnp.bfloat16)
    slot_rotation = jnp.dot(permuted, select.T, preferred_element_type=jnp.float32).astype(
        jnp.bfloat16
    )

    panel = lax.all_to_all(
        filtered.reshape(256, 8, 128), ("band", "gx", "gyz"), 0, 0, tiled=True
    )
    panel, slot_rotation = lax.optimization_barrier((panel, slot_rotation))
    panel = panel.reshape(256, 1024)
    margin = lax.dot_general(
        panel, panel, (((1,), (1,)), ((), ())), preferred_element_type=jnp.float32
    ) * (1.0 / total_cells)
    rows = margin.reshape(4, local_slots, total_slots)
    gram = lax.dynamic_index_in_dim(rows, band, 0, keepdims=False)
    for shift in range(1, 4):
        piece = lax.dynamic_index_in_dim(rows, lax.rem(band + shift, 4), 0, keepdims=False)
        gram = gram + to_band(piece.astype(jnp.bfloat16), shift).astype(jnp.float32)

    turned = lax.dot_general(
        slot_rotation, panel, (((0,), (0,)), ((), ())), preferred_element_type=jnp.float32
    ).astype(jnp.bfloat16)
    turned = turned.reshape(4, local_slots, total_slots * 4)
    rotated = jnp.zeros((local_slots, size_x, size_y, size_z), jnp.float32)

    def put(rotated, piece, shift):
        piece = piece.astype(jnp.float32).reshape(local_slots, 1, size_y, size_z)
        return lax.dynamic_update_slice_in_dim(rotated, piece, lax.rem(band + 4 - shift, 4), 1)

    def rows_for(shift):
        return lax.dynamic_index_in_dim(turned, lax.rem(band + shift, 4), 0, keepdims=False)

    rotated = put(rotated, rows_for(0), 0)
    second, first, third = (to_band(rows_for(shift), shift) for shift in (2, 1, 3))
    gram = reduce_over(gram, "gx", 2, 4)
    gram, second = lax.optimization_barrier((gram, second))
    gram = reduce_over(gram, "gyz", 2, 4)
    gram, first = lax.optimization_barrier((gram, first))
    gram = reduce_over(gram, "gyz", 1, 2)
    gram, third = lax.optimization_barrier((gram, third))
    gram = gram + lax.ppermute(gram, "gx", ACROSS)
    for shift, piece in ((2, second), (1, first), (3, third)):
        rotated = put(rotated, piece, shift)
    return (gram, rotated)


def solution(mesh):
    placed = (
        P("band", "gx", "gyz", None),
        P("gx", "gyz", None),
        P(None, "gx", "gyz", None),
        P(),
        P(),
        P(),
        P(),
        P(),
        P("band"),
    )
    return jax.shard_map(
        on_device,
        mesh=mesh,
        in_specs=placed,
        out_specs=(P("band", None), P("band", "gx", "gyz", None)),
        check_vma=False,
    )
```

```python
import jax
import jax.numpy as jnp
from jax import lax
from jax.experimental import pallas as pl
from jax.experimental.pallas import tpu as pltpu
from jax.sharding import PartitionSpec as P

DEG = 8


LOWER_EDGE = 2.0
CUT_EDGE = 3.0
UPPER_EDGE = 9.5


def coefficients(count):
    half_width = (UPPER_EDGE - CUT_EDGE) / 2.0
    centre = (UPPER_EDGE + CUT_EDGE) / 2.0
    first = half_width / (LOWER_EDGE - centre)
    factors = [(first / half_width, 0.0)]
    sigma = first
    for rounds in range(1, count):
        updated = 1.0 / (2.0 / first - sigma)
        factors.append((2.0 * updated / half_width, sigma * updated))
        sigma = updated
    return (factors, centre)


def silu(value):
    half = 0.5 * value
    return (half + half * jnp.tanh(half)).astype(jnp.bfloat16)


def network(cell_features, w_first, w_hidden, w_last):
    feature_count = cell_features.shape[0]
    flattened = cell_features.reshape(feature_count, -1)
    hidden = silu(jnp.dot(w_first, flattened, preferred_element_type=jnp.float32))
    hidden = silu(jnp.dot(w_hidden[0], hidden, preferred_element_type=jnp.float32))
    values = jnp.tanh(
        jnp.dot(
            jnp.broadcast_to(w_last, (8, w_last.shape[0])),
            hidden,
            preferred_element_type=jnp.float32,
        )[0]
    )
    return values.reshape(cell_features.shape[1:])


NX, NY, NZ = 32, 64, 128
PAD = 8
TOGETHER = 32
ORBITAL_SCALE = 8192.0
POTENTIAL_MIDDLE = 1.0


def filter_kernel(info, taken, other, out, field, shifted):
    factors, centre = coefficients(DEG)
    core = info[0]
    degree = info[1]
    edge = jnp.zeros((NY + 2 * PAD, NZ), jnp.float32)
    rim = jnp.zeros((PAD, NZ), jnp.float32)
    for which in range(2):
        field[which, 0] = edge
        field[which, NX + 1] = edge

    def load(outer, carry):
        for inner in range(4):
            plane = outer * 4 + inner
            for which in range(2):
                field[which, plane + 1, 0:PAD] = rim
                field[which, plane + 1, PAD + NY :] = rim
            for run in range(8):
                rows = slice(PAD + 8 * run, PAD + 8 * run + 8)
                field[0, plane + 1, rows] = taken[outer * 8 + run, inner] * (1.0 / ORBITAL_SCALE)
                own = taken[outer * 8 + run, 4 + inner % 2]
                far = other[outer * 8 + run, inner % 2]
                value = jnp.where(inner // 2 == core, own, far)
                shifted[plane, 8 * run : 8 * run + 8] = value + (POTENTIAL_MIDDLE + 3.0 - centre)
        return carry

    lax.fori_loop(0, NX // 4, load, 0)
    lane = lax.broadcasted_iota(jnp.int32, (8, NZ), 1)
    not_first = lane > 0
    not_last = lane < NZ - 1

    def tile(now, then, x, row, scale_new, scale_old):
        low = PAD + row
        here = field[now, x, low : low + 8]
        beside = field[now, x - 1, low : low + 8] + field[now, x + 1, low : low + 8]
        beside += field[now, x, low - 1 : low + 7] + field[now, x, low + 1 : low + 9]
        beside += jnp.where(not_first, pltpu.roll(here, 1, 1), 0.0) + jnp.where(
            not_last, pltpu.roll(here, NZ - 1, 1), 0.0
        )
        fresh = (scale_new * shifted[x - 1, row : row + 8]) * here - (0.5 * scale_new) * beside
        if scale_old != 0.0:
            fresh -= scale_old * field[then, x, low : low + 8]
        field[then, x, low : low + 8] = fresh

    for rounds in range(DEG):
        scale_new, scale_old = factors[rounds]
        now = rounds % 2

        @pl.when(rounds < degree)
        def _():
            def step(turn, carry):
                for part in range(TOGETHER):
                    for row in range(0, NY, 8):
                        tile(now, 1 - now, turn * TOGETHER + part + 1, row, scale_new, scale_old)
                return carry

            lax.fori_loop(0, NX // TOGETHER, step, 0)

    last = lax.rem(degree, 2)

    def store(outer, carry):
        for inner in range(4):
            out[inner, outer] = field[last, outer * 4 + inner + 1, PAD : PAD + NY].astype(
                jnp.bfloat16
            )
        return carry

    lax.fori_loop(0, NX // 4, store, 0)


ACROSS = [(i, i ^ 1) for i in range(8)]


def run_filter(info, taken, other):
    vmem = pl.BlockSpec(memory_space=pltpu.VMEM)
    return pl.pallas_call(
        filter_kernel,
        out_shape=jax.ShapeDtypeStruct((4, 8, NY, NZ), jnp.bfloat16),
        in_specs=[pl.BlockSpec(memory_space=pltpu.SMEM), vmem, vmem],
        out_specs=vmem,
        scratch_shapes=[
            pltpu.VMEM((2, NX + 2, NY + 2 * PAD, NZ), jnp.float32),
            pltpu.VMEM((NX, NY, NZ), jnp.float32),
        ],
        compiler_params=pltpu.CompilerParams(vmem_limit_bytes=24 * 1024 * 1024),
        cost_estimate=pl.CostEstimate(
            flops=8 * 16 * NX * NY * NZ, bytes_accessed=3 * 1024 * 1024, transcendentals=0
        ),
    )(info, taken, other)


def reduce_over(value, axis, step, count):
    size = lax.axis_size(axis)
    total = value
    sent = value.astype(jnp.bfloat16)
    for shift in range(1, count):
        pairs = []
        for i in range(size):
            place = (i // step) % count
            pairs.append((i, i + (((place + shift) % count) - place) * step))
        total = total + lax.ppermute(sent, axis, pairs).astype(value.dtype)
    return total


def to_band(value, shift):
    return lax.ppermute(value, "band", [(i, (i + shift) % 4) for i in range(4)])


def on_device(
    orbitals, v_local, features, w_first, w_hidden, w_last, rotation, assignment, degrees
):
    band = lax.axis_index("band")
    gx = lax.axis_index("gx")
    gyz = lax.axis_index("gyz")
    total_slots = rotation.shape[0]
    local_slots, size_x, size_y, size_z = orbitals.shape
    total_cells = float(NX * NY * NZ)

    potential = v_local + network(features, w_first, w_hidden, w_last)
    halves = potential.reshape(1, 2, 1, 2, size_y, size_z)
    halves = jnp.broadcast_to(halves, (4, 2, 8, 2, size_y, size_z)).reshape(64, 2, size_y, size_z)
    message = jnp.concatenate([orbitals * ORBITAL_SCALE, halves - POTENTIAL_MIDDLE], axis=1)
    message = message.astype(jnp.float16)
    core = lax.rem(gx, 2)
    degree = lax.dynamic_index_in_dim(degrees, gx * 8 + gyz, 0, keepdims=False)
    info = jnp.stack([core, degree]).astype(jnp.int32)
    taken = lax.all_to_all(message, ("gx", "gyz"), 0, 0, tiled=True)
    other = lax.ppermute(taken[:, 4:], "gx", ACROSS)
    filtered = run_filter(info, taken.astype(jnp.float32), other.astype(jnp.float32))

    select = (assignment[:, None] == lax.iota(jnp.int32, total_slots)[None, :]).astype(jnp.bfloat16)
    permuted = jnp.dot(
        select, rotation.astype(jnp.bfloat16), preferred_element_type=jnp.float32
    ).astype(jnp.bfloat16)
    slot_rotation = jnp.dot(permuted, select.T, preferred_element_type=jnp.float32).astype(
        jnp.bfloat16
    )

    panel = lax.all_to_all(
        filtered.reshape(256, 8, 128), ("band", "gx", "gyz"), 0, 0, tiled=True
    )
    panel, slot_rotation = lax.optimization_barrier((panel, slot_rotation))
    panel = panel.reshape(256, 1024)
    margin = lax.dot_general(
        panel, panel, (((1,), (1,)), ((), ())), preferred_element_type=jnp.float32
    ) * (1.0 / total_cells)
    rows = margin.reshape(4, local_slots, total_slots)
    gram = lax.dynamic_index_in_dim(rows, band, 0, keepdims=False)
    for shift in range(1, 4):
        piece = lax.dynamic_index_in_dim(rows, lax.rem(band + shift, 4), 0, keepdims=False)
        gram = gram + to_band(piece.astype(jnp.bfloat16), shift).astype(jnp.float32)

    turned = lax.dot_general(
        slot_rotation, panel, (((0,), (0,)), ((), ())), preferred_element_type=jnp.float32
    ).astype(jnp.bfloat16)
    turned = turned.reshape(4, local_slots, total_slots * 4)
    rotated = jnp.zeros((local_slots, size_x, size_y, size_z), jnp.float32)

    def put(rotated, piece, shift):
        piece = piece.astype(jnp.float32).reshape(local_slots, 1, size_y, size_z)
        return lax.dynamic_update_slice_in_dim(rotated, piece, lax.rem(band + 4 - shift, 4), 1)

    def rows_for(shift):
        return lax.dynamic_index_in_dim(turned, lax.rem(band + shift, 4), 0, keepdims=False)

    rotated = put(rotated, rows_for(0), 0)
    second = to_band(rows_for(2), 2)
    gram, leaving = lax.optimization_barrier((gram, rows_for(1)))
    first = to_band(leaving, 1)
    gram = reduce_over(gram, "gx", 2, 4)
    gram, second, leaving = lax.optimization_barrier((gram, second, rows_for(3)))
    third = to_band(leaving, 3)
    gram = reduce_over(gram, "gyz", 2, 4)
    gram, first = lax.optimization_barrier((gram, first))
    gram = reduce_over(gram, "gyz", 1, 2)
    gram, third = lax.optimization_barrier((gram, third))
    gram = gram + lax.ppermute(gram, "gx", ACROSS)
    for shift, piece in ((2, second), (1, first), (3, third)):
        rotated = put(rotated, piece, shift)
    return (gram, rotated)


def solution(mesh):
    placed = (
        P("band", "gx", "gyz", None),
        P("gx", "gyz", None),
        P(None, "gx", "gyz", None),
        P(),
        P(),
        P(),
        P(),
        P(),
        P("band"),
    )
    return jax.shard_map(
        on_device,
        mesh=mesh,
        in_specs=placed,
        out_specs=(P("band", None), P("band", "gx", "gyz", None)),
        check_vma=False,
    )
```

```python
import jax
import jax.numpy as jnp
from jax import lax
from jax.experimental import pallas as pl
from jax.experimental.pallas import tpu as pltpu
from jax.sharding import PartitionSpec as P

DEG = 8


LOWER_EDGE = 2.0
CUT_EDGE = 3.0
UPPER_EDGE = 9.5


def coefficients(count):
    half_width = (UPPER_EDGE - CUT_EDGE) / 2.0
    centre = (UPPER_EDGE + CUT_EDGE) / 2.0
    first = half_width / (LOWER_EDGE - centre)
    factors = [(first / half_width, 0.0)]
    sigma = first
    for rounds in range(1, count):
        updated = 1.0 / (2.0 / first - sigma)
        factors.append((2.0 * updated / half_width, sigma * updated))
        sigma = updated
    return (factors, centre)


def silu(value):
    half = 0.5 * value
    return (half + half * jnp.tanh(half)).astype(jnp.bfloat16)


def network(cell_features, w_first, w_hidden, w_last):
    feature_count = cell_features.shape[0]
    flattened = cell_features.reshape(feature_count, -1)
    hidden = silu(jnp.dot(w_first, flattened, preferred_element_type=jnp.float32))
    hidden = silu(jnp.dot(w_hidden[0], hidden, preferred_element_type=jnp.float32))
    values = jnp.tanh(
        jnp.dot(
            jnp.broadcast_to(w_last, (8, w_last.shape[0])),
            hidden,
            preferred_element_type=jnp.float32,
        )[0]
    )
    return values.reshape(cell_features.shape[1:])


NX, NY, NZ = 32, 64, 128
PAD = 8
TOGETHER = 32
ORBITAL_SCALE = 8192.0
POTENTIAL_MIDDLE = 1.0


def filter_kernel(info, taken, other, out, field, shifted):
    factors, centre = coefficients(DEG)
    core = info[0]
    degree = info[1]
    edge = jnp.zeros((NY + 2 * PAD, NZ), jnp.float32)
    rim = jnp.zeros((PAD, NZ), jnp.float32)
    for which in range(2):
        field[which, 0] = edge
        field[which, NX + 1] = edge

    def load(outer, carry):
        for inner in range(4):
            plane = outer * 4 + inner
            for which in range(2):
                field[which, plane + 1, 0:PAD] = rim
                field[which, plane + 1, PAD + NY :] = rim
            for run in range(8):
                rows = slice(PAD + 8 * run, PAD + 8 * run + 8)
                field[0, plane + 1, rows] = taken[outer * 8 + run, inner] * (1.0 / ORBITAL_SCALE)
                own = taken[outer * 8 + run, 4 + inner % 2]
                far = other[outer * 8 + run, inner % 2]
                value = jnp.where(inner // 2 == core, own, far)
                shifted[plane, 8 * run : 8 * run + 8] = value + (POTENTIAL_MIDDLE + 3.0 - centre)
        return carry

    lax.fori_loop(0, NX // 4, load, 0)
    lane = lax.broadcasted_iota(jnp.int32, (8, NZ), 1)
    not_first = lane > 0
    not_last = lane < NZ - 1

    def tile(now, then, x, row, scale_new, scale_old):
        low = PAD + row
        here = field[now, x, low : low + 8]
        beside = field[now, x - 1, low : low + 8] + field[now, x + 1, low : low + 8]
        beside += field[now, x, low - 1 : low + 7] + field[now, x, low + 1 : low + 9]
        beside += jnp.where(not_first, pltpu.roll(here, 1, 1), 0.0) + jnp.where(
            not_last, pltpu.roll(here, NZ - 1, 1), 0.0
        )
        fresh = (scale_new * shifted[x - 1, row : row + 8]) * here - (0.5 * scale_new) * beside
        if scale_old != 0.0:
            fresh -= scale_old * field[then, x, low : low + 8]
        field[then, x, low : low + 8] = fresh

    for rounds in range(DEG):
        scale_new, scale_old = factors[rounds]
        now = rounds % 2

        @pl.when(rounds < degree)
        def _():
            def step(turn, carry):
                for part in range(TOGETHER):
                    for row in range(0, NY, 8):
                        tile(now, 1 - now, turn * TOGETHER + part + 1, row, scale_new, scale_old)
                return carry

            lax.fori_loop(0, NX // TOGETHER, step, 0)

    last = lax.rem(degree, 2)

    def store(outer, carry):
        for inner in range(4):
            out[inner, outer] = field[last, outer * 4 + inner + 1, PAD : PAD + NY].astype(
                jnp.bfloat16
            )
        return carry

    lax.fori_loop(0, NX // 4, store, 0)


ACROSS = [(i, i ^ 1) for i in range(8)]


def run_filter(info, taken, other):
    vmem = pl.BlockSpec(memory_space=pltpu.VMEM)
    return pl.pallas_call(
        filter_kernel,
        out_shape=jax.ShapeDtypeStruct((4, 8, NY, NZ), jnp.bfloat16),
        in_specs=[pl.BlockSpec(memory_space=pltpu.SMEM), vmem, vmem],
        out_specs=vmem,
        scratch_shapes=[
            pltpu.VMEM((2, NX + 2, NY + 2 * PAD, NZ), jnp.float32),
            pltpu.VMEM((NX, NY, NZ), jnp.float32),
        ],
        compiler_params=pltpu.CompilerParams(vmem_limit_bytes=24 * 1024 * 1024),
        cost_estimate=pl.CostEstimate(
            flops=8 * 16 * NX * NY * NZ, bytes_accessed=3 * 1024 * 1024, transcendentals=0
        ),
    )(info, taken, other)


def reduce_over(value, axis, step, count):
    size = lax.axis_size(axis)
    total = value
    sent = value.astype(jnp.bfloat16)
    for shift in range(1, count):
        pairs = []
        for i in range(size):
            place = (i // step) % count
            pairs.append((i, i + (((place + shift) % count) - place) * step))
        total = total + lax.ppermute(sent, axis, pairs).astype(value.dtype)
    return total


def to_band(value, shift):
    return lax.ppermute(value, "band", [(i, (i + shift) % 4) for i in range(4)])


def on_device(
    orbitals, v_local, features, w_first, w_hidden, w_last, rotation, assignment, degrees
):
    band = lax.axis_index("band")
    gx = lax.axis_index("gx")
    gyz = lax.axis_index("gyz")
    total_slots = rotation.shape[0]
    local_slots, size_x, size_y, size_z = orbitals.shape
    total_cells = float(NX * NY * NZ)

    potential = v_local + network(features, w_first, w_hidden, w_last)
    halves = potential.reshape(1, 2, 1, 2, size_y, size_z)
    halves = jnp.broadcast_to(halves, (4, 2, 8, 2, size_y, size_z)).reshape(64, 2, size_y, size_z)
    message = jnp.concatenate([orbitals * ORBITAL_SCALE, halves - POTENTIAL_MIDDLE], axis=1)
    message = message.astype(jnp.float16)
    core = lax.rem(gx, 2)
    degree = lax.dynamic_index_in_dim(degrees, gx * 8 + gyz, 0, keepdims=False)
    info = jnp.stack([core, degree]).astype(jnp.int32)
    taken = lax.all_to_all(message, ("gx", "gyz"), 0, 0, tiled=True)
    other = lax.ppermute(taken[:, 4:], "gx", ACROSS)
    filtered = run_filter(info, taken.astype(jnp.float32), other.astype(jnp.float32))

    select = (assignment[:, None] == lax.iota(jnp.int32, total_slots)[None, :]).astype(jnp.bfloat16)
    permuted = jnp.dot(
        select, rotation.astype(jnp.bfloat16), preferred_element_type=jnp.float32
    ).astype(jnp.bfloat16)
    slot_rotation = jnp.dot(permuted, select.T, preferred_element_type=jnp.float32).astype(
        jnp.bfloat16
    )

    panel = lax.all_to_all(
        filtered.reshape(256, 8, 128), ("band", "gx", "gyz"), 0, 0, tiled=True
    )
    panel, slot_rotation = lax.optimization_barrier((panel, slot_rotation))
    panel = panel.reshape(256, 1024)
    margin = lax.dot_general(
        panel, panel, (((1,), (1,)), ((), ())), preferred_element_type=jnp.float32
    ) * (1.0 / total_cells)
    rows = margin.reshape(4, local_slots, total_slots)
    gram = lax.dynamic_index_in_dim(rows, band, 0, keepdims=False)
    for shift in range(1, 4):
        piece = lax.dynamic_index_in_dim(rows, lax.rem(band + shift, 4), 0, keepdims=False)
        gram = gram + to_band(piece.astype(jnp.bfloat16), shift).astype(jnp.float32)

    turned = lax.dot_general(
        slot_rotation, panel, (((0,), (0,)), ((), ())), preferred_element_type=jnp.float32
    ).astype(jnp.bfloat16)
    turned = turned.reshape(4, local_slots, total_slots * 4)
    rotated = jnp.zeros((local_slots, size_x, size_y, size_z), jnp.float32)

    def put(rotated, piece, shift):
        piece = piece.astype(jnp.float32).reshape(local_slots, 1, size_y, size_z)
        return lax.dynamic_update_slice_in_dim(rotated, piece, lax.rem(band + 4 - shift, 4), 1)

    def rows_for(shift):
        return lax.dynamic_index_in_dim(turned, lax.rem(band + shift, 4), 0, keepdims=False)

    rotated = put(rotated, rows_for(0), 0)
    second = to_band(rows_for(2), 2)
    gram, leaving = lax.optimization_barrier((gram, rows_for(1)))
    first = to_band(leaving, 1)
    gram = reduce_over(gram, "gx", 2, 4)
    gram, second, leaving = lax.optimization_barrier((gram, second, rows_for(3)))
    third = to_band(leaving, 3)
    gram = reduce_over(gram, "gyz", 2, 4)
    gram, first = lax.optimization_barrier((gram, first))
    sent = gram.astype(jnp.bfloat16)
    others = [
        lax.ppermute(sent, ("gx", "gyz"), [(i, i ^ flip) for i in range(64)]) for flip in (9, 1, 8)
    ]
    others[0], third = lax.optimization_barrier((others[0], third))
    gram = gram + sum(other.astype(jnp.float32) for other in others)
    for shift, piece in ((2, second), (1, first), (3, third)):
        rotated = put(rotated, piece, shift)
    return (gram, rotated)


def solution(mesh):
    placed = (
        P("band", "gx", "gyz", None),
        P("gx", "gyz", None),
        P(None, "gx", "gyz", None),
        P(),
        P(),
        P(),
        P(),
        P(),
        P("band"),
    )
    return jax.shard_map(
        on_device,
        mesh=mesh,
        in_specs=placed,
        out_specs=(P("band", None), P("band", "gx", "gyz", None)),
        check_vma=False,
    )
```
